256 devices in a mesh: row: 16 (over z, core), col: 16 (over x, y).
Axes of the slice: x: 4, y: 4, z: 8, core: 2. Of those that a mesh axis runs over, the one named last changes fastest.
Arguments:
- matrix: float32 [2, 16, 512, 2, 16, 512], P(None, 'row', None, None, 'col'), may hold values from 0 to 34, as said below
Outputs:
- factored: float32 [2, 16, 512, 2, 16, 512], P(None, 'row', None, None, 'col')
The draws below stay inside these ranges and needn't reach their ends.
Inputs may be any that keep to these rules, and one draw needn't show every extreme that they name: matrix is symmetric and positive definite, with all entries positive.
All inputs are finite; a program needn't handle non-finite values.
Results may differ from the reference program's by a relative error of at most 0.0003.
Values sent between devices are 32-bit elements; how exact they have to be, the bound alone decides.
A program may use at most 128 MiB of HBM per device.

```python
import math
import jax
import jax.numpy as jnp
from jax import lax

NB = 512
TPD = 2
KC = 2
ORDER = 16384


def draw_matrix(key, part):
    key = jax.random.fold_in(key, 11)
    key_points, key_scale = jax.random.split(key)
    points = jax.random.uniform(key_points, (ORDER, 3), jnp.float32)
    scale = jnp.exp(jax.random.uniform(key_scale, (ORDER,), jnp.float32, math.log(0.4), math.log(4.0)))
    length = 0.25
    squared = (points[:, 0][:, None] - points[:, 0][None, :]) ** 2
    squared = squared + (points[:, 1][:, None] - points[:, 1][None, :]) ** 2
    squared = squared + (points[:, 2][:, None] - points[:, 2][None, :]) ** 2
    kernel = jnp.exp(-jnp.sqrt(squared) / length)
    identity = (lax.broadcasted_iota(jnp.int32, (ORDER, ORDER), 0) == lax.broadcasted_iota(jnp.int32, (ORDER, ORDER), 1)).astype(jnp.float32)
    matrix_full = scale[:, None] * scale[None, :] * (kernel + identity)
    grid_rows = ORDER // NB // TPD
    grid_cols = ORDER // NB // KC
    return matrix_full.reshape(TPD, grid_rows, NB, KC, grid_cols, NB)


def setup_inputs(seed: int = 0) -> dict:
    keys = jax.random.split(jax.random.key(seed), 2)
    matrix = draw_matrix(jax.random.fold_in(keys[1], 71), 0)
    return {"matrix": matrix}


def reference(matrix):
    matrix_full = matrix.reshape(ORDER, ORDER)
    for panel in range(2):
        start_row = panel * NB
        end_row = start_row + NB
        factor = jnp.tril(jnp.linalg.cholesky(matrix_full[start_row:end_row, start_row:end_row]))
        beneath = jax.scipy.linalg.solve_triangular(factor, matrix_full[end_row:, start_row:end_row].T, lower=True).T
        column_new = jnp.concatenate([jnp.zeros((start_row, NB), jnp.float32), factor, beneath], 0)
        matrix_full = matrix_full.at[:, start_row:end_row].set(column_new)
        matrix_full = matrix_full.at[start_row:end_row, end_row:].set(0.0)
        product = jnp.dot(beneath.astype(jnp.float32), beneath.T.astype(jnp.float32), precision=lax.Precision.HIGHEST, preferred_element_type=jnp.float32)
        matrix_full = matrix_full.at[end_row:, end_row:].set(matrix_full[end_row:, end_row:] - product)
    return matrix_full.reshape(matrix.shape)
```

```python
import jax
import jax.numpy as jnp
from jax import lax
from jax.experimental import pallas as pl
from jax.experimental.pallas import tpu as pltpu
from jax.sharding import PartitionSpec as P

F32 = jnp.float32
BF16 = jnp.bfloat16
MESH = pl.DeviceIdType.MESH
NN = (((1,), (0,)), ((), ()))
NT = (((1,), (1,)), ((), ()))
Z = 8
J = 16
T = 512
B = 128


def split(x):
    high = x.astype(BF16)
    return high, (x - high.astype(F32)).astype(BF16)


def dot3(a, b, dims=NN):
    def one(x, y):
        return lax.dot_general(x, y, dims, preferred_element_type=F32)

    return one(a[0], b[0]) + (one(a[0], b[1]) + one(a[1], b[0]))


def lane(x, i):
    return jnp.take_along_axis(x, jnp.full((8, 128), i, jnp.int32), axis=1)


def sublane(x, i):
    return jnp.broadcast_to(x[i : i + 1, :], (8, 128))


def factor_block(s_ref, u_ref, w_ref):
    n = B // 8
    s = [s_ref[8 * i : 8 * i + 8, :] for i in range(n)]
    row = lax.broadcasted_iota(jnp.int32, (8, 128), 0)
    col = lax.broadcasted_iota(jnp.int32, (8, 128), 1)
    v = [(col == row + 8 * i).astype(F32) for i in range(n)]
    for g in range(n):
        a = [sublane(s[g], j) for j in range(8)]
        x = [sublane(v[g], j) for j in range(8)]
        d = {}
        for i in range(8):
            for j in range(i + 1):
                d[i, j] = lane(a[j], 8 * g + i)
        inv = [None] * 8
        low = {}
        for j in range(8):
            inv[j] = 1.0 / d[j, j]
            for i in range(j + 1, 8):
                low[i, j] = d[i, j] * inv[j]
            for i in range(j + 1, 8):
                for k in range(j + 1, i + 1):
                    d[i, k] = d[i, k] - low[i, j] * d[k, j]
                a[i] = a[i] - low[i, j] * a[j]
                x[i] = x[i] - low[i, j] * x[j]
        scale = lax.rsqrt(d[7, 7])
        u_out = a[7] * scale
        w_out = x[7] * scale
        for j in range(7):
            scale = lax.rsqrt(d[j, j])
            u_out = jnp.where(row == j, a[j] * scale, u_out)
            w_out = jnp.where(row == j, x[j] * scale, w_out)
        u_ref[8 * g : 8 * g + 8, :] = jnp.where(col >= row + 8 * g, u_out, 0.0)
        w_ref[8 * g : 8 * g + 8, :] = w_out
        if g == n - 1:
            break
        y = [None] * 8
        p = [None] * 8
        for j in range(7, -1, -1):
            y[j] = a[j] * inv[j]
            p[j] = x[j] * inv[j]
            for i in range(7, j, -1):
                y[j] = y[j] - low[i, j] * y[i]
                p[j] = p[j] - low[i, j] * p[i]
        for r in range(g + 1, n):
            old = s[r]
            for j in range(7, -1, -1):
                c = lane(old, 8 * g + j)
                s[r] = s[r] - c * y[j]
                v[r] = v[r] - c * p[j]


STAGES = ((0, 0, 8, 0, 0), (0, 128, 24, 0, 0), (1, 0, 32, 1, 0), (2, 0, 32, 1, 1))


def kernel(
    a_hbm,
    o_hbm,
    mine,
    rp,
    cp,
    dt,
    s_blk,
    u_blk,
    w_blk,
    lo,
    w,
    w_h,
    w_l,
    up,
    up_h,
    up_l,
    un_h,
    un_l,
    xr,
    xr_h,
    xr_l,
    xc_h,
    xc_l,
    io_sem,
    d1s,
    d1r,
    d2s,
    d2r,
    d3s,
    d3r,
    d4s,
    d4r,
    r1s,
    r1r,
    r2s,
    r2r,
    c1s,
    c1r,
    c2s,
    c2r,
    c3s,
    c3r,
):
    r = lax.axis_index("row")
    q = lax.axis_index("col")
    z = r // 2
    core = lax.rem(r, 2)
    other = r + 1 - 2 * core

    def send(ref, send_sem, recv_sem, device):
        return pltpu.make_async_remote_copy(
            src_ref=ref,
            dst_ref=ref,
            send_sem=send_sem,
            recv_sem=recv_sem,
            device_id=device,
            device_id_type=MESH,
        )

    load = pltpu.make_async_copy(a_hbm, mine, io_sem.at[0])
    load.start()

    barrier = pltpu.get_barrier_semaphore()

    def greet(device):
        pl.semaphore_signal(barrier, inc=1, device_id=device, device_id_type=MESH)

    @pl.loop(1, J)
    def _(k):
        greet((r, lax.rem(q + k, J)))

    @pl.loop(1, Z)
    def _(k):
        greet((lax.rem(r + 2 * k, 2 * Z), q))

    greet((other, q))
    load.wait()

    def tile_col(i, m, b, count=T):
        return mine[pl.ds(i * T * 8 + m * 4 + b, count, stride=8), :]

    @pl.when(q < 2)
    def _():
        @pl.loop(0, 2)
        def _(i):
            for b in range(4):
                rp[q, pl.ds(pl.multiple_of(i * T, T), T), b * B : (b + 1) * B] = tile_col(i, 0, b)

    @pl.when(z == 0)
    def _():
        for m in range(2):
            for b in range(4):
                at = (m * 4 + b) * B
                cp[pl.ds(pl.multiple_of(core * T, T), T), at : at + B] = tile_col(0, m, b)

    for t, (dr, dq) in enumerate(((0, 0), (0, 1), (1, 1))):

        @pl.when((r == dr) & (q == dq))
        def _():
            for b in range(4):
                dt[t, :, b * B : (b + 1) * B] = tile_col(0, 0, b)

    pl.semaphore_wait(barrier, (J - 1) + (Z - 1) + 1)

    def piece(n, j):
        t, first, rows, _, _ = STAGES[n]
        return dt.at[t, pl.ds(pl.multiple_of(first + j * rows, 8), rows), :]

    def whole(n):
        t, first, rows, _, _ = STAGES[n]
        return dt.at[t, pl.ds(first, rows * J), :]

    def d1(n, j):
        return send(piece(n, j), d1s.at[n, j], d1r.at[n], (r, j))

    def d2(n, k):
        return send(piece(n, q), d2s.at[n, k], d2r.at[n], (2 * k + core, q))

    def d3(n, j, sender):
        return send(piece(n, sender), d3s.at[n, j], d3r.at[n, sender], (r, j))

    def d4(n):
        return send(whole(n), d4s.at[n], d4r.at[n], (other, q))

    def is_source(n):
        return (z == 0) & (q == STAGES[n][3])

    def d_scatter(n, act):
        @pl.when((core == STAGES[n][4]) & is_source(n))
        def _():
            @pl.loop(0, J)
            def _(j):
                @pl.when(j != q)
                def _():
                    act(d1(n, j))

    def d_along_z(n, act):
        @pl.when((core == STAGES[n][4]) & (z == 0))
        def _():
            @pl.loop(1, Z)
            def _(k):
                act(d2(n, k))

    def d_gather(n, act):
        @pl.when(core == STAGES[n][4])
        def _():
            @pl.loop(0, J)
            def _(j):
                @pl.when((j != q) & ((z != 0) | (j != STAGES[n][3])))
                def _():
                    act(d3(n, j, q))

    def start(copy):
        copy.start()

    def sent(copy):
        copy.wait_send()

    def d_step2(n):
        @pl.when((core == STAGES[n][4]) & (z == 0) & (q != STAGES[n][3]))
        def _():
            d1(n, q).wait_recv()

        d_along_z(n, start)

    def d_step3(n):
        @pl.when((core == STAGES[n][4]) & (z != 0))
        def _():
            d2(n, 0).wait_recv()

        d_gather(n, start)

    def d_step4(n):
        @pl.when(core == STAGES[n][4])
        def _():
            @pl.when(jnp.logical_not(is_source(n)))
            def _():
                @pl.loop(0, J)
                def _(j):
                    @pl.when(j != q)
                    def _():
                        d3(n, 0, j).wait_recv()

            d4(n).start()

        @pl.when(core != STAGES[n][4])
        def _():
            d4(n).wait_recv()

    def d_finish(n):
        d_scatter(n, sent)
        d_along_z(n, sent)
        d_gather(n, sent)

        @pl.when(core == STAGES[n][4])
        def _():
            d4(n).wait_send()

    def r_piece(s, j):
        return rp.at[s, pl.ds(pl.multiple_of(j * 64, 64), 64), :]

    def r1(s, j):
        return send(r_piece(s, j), r1s.at[s, j], r1r.at[s], (r, j))

    def r2(s, j, sender):
        return send(r_piece(s, sender), r2s.at[s, j], r2r.at[s, sender], (r, j))

    def r_scatter(act):
        for s in range(2):

            @pl.when(q == s)
            def _():
                @pl.loop(0, J)
                def _(j):
                    @pl.when(j != s)
                    def _():
                        act(r1(s, j))

    def r_gather(s, act):
        @pl.loop(0, J)
        def _(j):
            @pl.when((j != q) & (j != s))
            def _():
                act(r2(s, j, q))

    def r_step2(s):
        @pl.when(q != s)
        def _():
            r1(s, q).wait_recv()

        r_gather(s, start)

    def r_arrive(s):
        @pl.when(q != s)
        def _():
            @pl.loop(0, J)
            def _(j):
                @pl.when(j != q)
                def _():
                    r2(s, 0, j).wait_recv()

    def c_piece(half, k):
        return cp.at[pl.ds(pl.multiple_of(half * T + k * 64, 64), 64), :]

    def c1(k):
        return send(c_piece(core, k), c1s.at[k], c1r.at[0], (2 * k + core, q))

    def c2(k, sender):
        return send(c_piece(core, sender), c2s.at[k], c2r.at[sender], (2 * k + core, q))

    def c3(half, k):
        return send(c_piece(half, k), c3s.at[k], c3r.at[k], (other, q))

    def c_scatter(act):
        @pl.when(z == 0)
        def _():
            @pl.loop(1, Z)
            def _(k):
                act(c1(k))

    def c_gather(act):
        @pl.loop(1, Z)
        def _(k):
            @pl.when(k != z)
            def _():
                act(c2(k, z))

    def c_step2():
        @pl.when(z != 0)
        def _():
            c1(z).wait_recv()

        c_gather(start)

    def c_step3():
        @pl.loop(0, Z)
        def _(k):
            @pl.when((z != 0) & (k != z))
            def _():
                c2(0, k).wait_recv()

            c3(core, k).start()

    def c_arrive():
        @pl.loop(0, Z)
        def _(k):
            c3(1 - core, k).wait_recv()

    for n in range(4):
        d_scatter(n, start)
    r_scatter(start)
    c_scatter(start)
    d_step2(0)
    d_step3(0)
    d_step2(1)
    d_step4(0)

    lo[...] = jnp.zeros_like(lo)
    w[...] = jnp.zeros_like(w)

    @pl.loop(0, 2)
    def _(h):
        tile = 3 * h
        for k in range(4):
            at, end = k * B, (k + 1) * B
            rows = dt[tile, at:end, at:T]
            if k:
                left = split(lo[at:end, 0:at])
                rows = rows - dot3(left, split(up[0:at, at:T]))
            s_blk[...] = rows[:, 0:B]
            factor_block(s_blk, u_blk, w_blk)
            w_kk = split(w_blk[...])
            w[h, at:end, at:end] = w_blk[...]
            if k:
                inner = dot3(left, split(w[h, 0:at, 0:at]))
                w[h, at:end, 0:at] = -dot3(w_kk, split(inner))
            if k < 3:
                beside = dot3(w_kk, split(rows[:, B:]))
                up[at:end, end:T] = beside
                lo[end:T, at:end] = beside.T
            if k == 0:

                @pl.when(h == 0)
                def _():
                    d_step3(1)
                    d_step2(2)
                    d_step2(3)
                    r_step2(0)
                    c_step2()
                    d_step4(1)

            if k == 1:

                @pl.when(h == 0)
                def _():
                    d_step3(2)
                    d_step3(3)
                    r_step2(1)

                @pl.when(h == 1)
                def _():
                    c_step3()

        whole_w = split(w[h])
        w_h[h] = whole_w[0]
        w_l[h] = whole_w[1]

        @pl.when(h == 0)
        def _():
            d_step4(2)
            d_step4(3)
            over = dot3(whole_w, split(dt[1]))
            over_s = split(over)
            under_s = split(over.T)
            up_h[...], up_l[...] = over_s
            un_h[...], un_l[...] = under_s
            dt[3] = dt[2] - dot3(under_s, over_s)

    r_arrive(0)
    r_arrive(1)

    w0 = (w_h[0], w_l[0])
    w1 = (w_h[1], w_l[1])
    over = (up_h[...], up_l[...])
    under = (un_h[...], un_l[...])

    @pl.loop(0, 2)
    def _(i):
        rows = pl.ds(pl.multiple_of(i * T, T), T)
        x0 = dot3(split(rp[0, rows, :]), w0, NT)
        x0_s = split(x0)
        xr[rows, 0:T] = x0
        xr_h[rows, 0:T], xr_l[rows, 0:T] = x0_s
        rest = rp[1, rows, :] - dot3(x0_s, over)
        x1 = dot3(split(rest), w1, NT)
        xr[rows, T:] = x1
        xr_h[rows, T:], xr_l[rows, T:] = split(x1)

    c_arrive()

    @pl.loop(0, 2)
    def _(m):
        cols = pl.ds(pl.multiple_of(m * T, T), T)
        x0_s = split(dot3(w0, split(cp[0:T, cols])))
        xc_h[0:T, cols], xc_l[0:T, cols] = x0_s
        rest = cp[T:, cols] - dot3(under, x0_s)
        xc_h[T:, cols], xc_l[T:, cols] = split(dot3(w1, split(rest)))

    at_row = lax.broadcasted_iota(jnp.int32, (T, T), 0)
    at_col = lax.broadcasted_iota(jnp.int32, (T, T), 1)

    @pl.loop(0, 2)
    def _(i):
        rows = pl.ds(pl.multiple_of(i * T, T), T)

        def put(m, value, update):
            for b in range(4):
                place = pl.ds(i * T * 8 + m * 4 + b, T, stride=8)
                part = value[:, b * B : (b + 1) * B]
                mine[place, :] = mine[place, :] - part if update else part

        row_tile = r + J * i

        @pl.loop(0, 2)
        def _(m):
            cols = pl.ds(pl.multiple_of(m * T, T), T)
            col_tile = q + J * m

            @pl.when((col_tile >= 2) & (row_tile >= 2))
            def _():
                put(m, dot3((xr_h[rows, :], xr_l[rows, :]), (xc_h[:, cols], xc_l[:, cols])), True)

            @pl.when((col_tile >= 2) & (row_tile < 2))
            def _():
                put(m, jnp.zeros((T, T), F32), False)

            @pl.when(col_tile < 2)
            def _():
                value = xr[rows, pl.ds(pl.multiple_of(col_tile * T, T), T)]
                keep = (row_tile > col_tile) | ((row_tile == col_tile) & (at_row >= at_col))
                put(m, jnp.where(keep, value, 0.0), False)

        block = pl.ds(pl.multiple_of(i * T * 8, T * 8), T * 8)
        pltpu.make_async_copy(mine.at[block], o_hbm.at[block], io_sem.at[1 + i]).start()

    for n in range(4):
        d_finish(n)
    r_scatter(sent)
    r_gather(0, sent)
    r_gather(1, sent)
    c_scatter(sent)
    c_gather(sent)

    @pl.loop(0, Z)
    def _(k):
        c3(core, k).wait_send()

    @pl.loop(0, 2)
    def _(i):
        block = pl.ds(pl.multiple_of(i * T * 8, T * 8), T * 8)
        pltpu.make_async_copy(mine.at[block], o_hbm.at[block], io_sem.at[1 + i]).wait()


def body(matrix):
    local = matrix.reshape(8192, 128)
    dma = pltpu.SemaphoreType.DMA
    out = pl.pallas_call(
        kernel,
        out_shape=jax.ShapeDtypeStruct((8192, 128), F32),
        in_specs=[pl.BlockSpec(memory_space=pl.ANY)],
        out_specs=pl.BlockSpec(memory_space=pl.ANY),
        scratch_shapes=[
            pltpu.VMEM((8192, 128), F32),
            pltpu.VMEM((2, 2 * T, T), F32),
            pltpu.VMEM((2 * T, 2 * T), F32),
            pltpu.VMEM((4, T, T), F32),
            pltpu.VMEM((B, B), F32),
            pltpu.VMEM((B, B), F32),
            pltpu.VMEM((B, B), F32),
            pltpu.VMEM((T, T), F32),
            pltpu.VMEM((2, T, T), F32),
            pltpu.VMEM((2, T, T), BF16),
            pltpu.VMEM((2, T, T), BF16),
            pltpu.VMEM((T, T), F32),
            pltpu.VMEM((T, T), BF16),
            pltpu.VMEM((T, T), BF16),
            pltpu.VMEM((T, T), BF16),
            pltpu.VMEM((T, T), BF16),
            pltpu.VMEM((2 * T, 2 * T), F32),
            pltpu.VMEM((2 * T, 2 * T), BF16),
            pltpu.VMEM((2 * T, 2 * T), BF16),
            pltpu.VMEM((2 * T, 2 * T), BF16),
            pltpu.VMEM((2 * T, 2 * T), BF16),
            dma((3,)),
            dma((4, J)),
            dma((4,)),
            dma((4, Z)),
            dma((4,)),
            dma((4, J)),
            dma((4, J)),
            dma((4,)),
            dma((4,)),
            dma((2, J)),
            dma((2,)),
            dma((2, J)),
            dma((2, J)),
            dma((Z,)),
            dma((1,)),
            dma((Z,)),
            dma((Z,)),
            dma((Z,)),
            dma((Z,)),
        ],
        compiler_params=pltpu.CompilerParams(
            collective_id=0, has_side_effects=True, vmem_limit_bytes=56 * 1024 * 1024
        ),
        cost_estimate=pl.CostEstimate(
            flops=30_000_000_000, bytes_accessed=8 * 1024 * 1024, transcendentals=0
        ),
        name="panels",
    )(local)
    return out.reshape(matrix.shape)


def solution(mesh):
    return jax.shard_map(
        body,
        mesh=mesh,
        in_specs=(P(None, "row", None, None, "col", None),),
        out_specs=P(None, "row", None, None, "col", None),
        check_vma=False,
    )
```

```python
import jax
import jax.numpy as jnp
from jax import lax
from jax.experimental import pallas as pl
from jax.experimental.pallas import tpu as pltpu
from jax.sharding import PartitionSpec as P

F32 = jnp.float32
BF16 = jnp.bfloat16
MESH = pl.DeviceIdType.MESH
NN = (((1,), (0,)), ((), ()))
NT = (((1,), (1,)), ((), ()))
Z = 8
J = 16
T = 512
B = 128
CHUNKS = 16
LAG = 4
EARLY = 2


def split(x):
    high = x.astype(BF16)
    return high, (x - high.astype(F32)).astype(BF16)


def dot3(a, b, dims=NN):
    def one(x, y):
        return lax.dot_general(x, y, dims, preferred_element_type=F32)

    return one(a[0], b[0]) + (one(a[0], b[1]) + one(a[1], b[0]))


def lane(x, i):
    return jnp.take_along_axis(x, jnp.full((8, 128), i, jnp.int32), axis=1)


def sublane(x, i):
    return jnp.broadcast_to(x[i : i + 1, :], (8, 128))


def factor_block(s_ref, u_ref, w_ref, between):
    n = B // 8
    s = [s_ref[8 * i : 8 * i + 8, :] for i in range(n)]
    row = lax.broadcasted_iota(jnp.int32, (8, 128), 0)
    col = lax.broadcasted_iota(jnp.int32, (8, 128), 1)
    v = [(col == row + 8 * i).astype(F32) for i in range(n)]
    for g in range(n):
        if g % 4 == 0:
            between(g // 4)
        a = [sublane(s[g], j) for j in range(8)]
        x = [sublane(v[g], j) for j in range(8)]
        d = {}
        for i in range(8):
            for j in range(i + 1):
                d[i, j] = lane(a[j], 8 * g + i)
        inv = [None] * 8
        low = {}
        for j in range(8):
            inv[j] = 1.0 / d[j, j]
            for i in range(j + 1, 8):
                low[i, j] = d[i, j] * inv[j]
            for i in range(j + 1, 8):
                for k in range(j + 1, i + 1):
                    d[i, k] = d[i, k] - low[i, j] * d[k, j]
                a[i] = a[i] - low[i, j] * a[j]
                x[i] = x[i] - low[i, j] * x[j]
        scale = lax.rsqrt(d[7, 7])
        u_out = a[7] * scale
        w_out = x[7] * scale
        for j in range(7):
            scale = lax.rsqrt(d[j, j])
            u_out = jnp.where(row == j, a[j] * scale, u_out)
            w_out = jnp.where(row == j, x[j] * scale, w_out)
        u_ref[8 * g : 8 * g + 8, :] = jnp.where(col >= row + 8 * g, u_out, 0.0)
        w_ref[8 * g : 8 * g + 8, :] = w_out
        if g == n - 1:
            break
        y = [None] * 8
        p = [None] * 8
        for j in range(7, -1, -1):
            y[j] = a[j] * inv[j]
            p[j] = x[j] * inv[j]
            for i in range(7, j, -1):
                y[j] = y[j] - low[i, j] * y[i]
                p[j] = p[j] - low[i, j] * p[i]
        for r in range(g + 1, n):
            old = s[r]
            for j in range(7, -1, -1):
                c = lane(old, 8 * g + j)
                s[r] = s[r] - c * y[j]
                v[r] = v[r] - c * p[j]


AROUND = (
    ((1, 0), (0, 1), (3, 0), (0, 3), (1, 1), (0, 2), (3, 1), (2, 0))
    + ((1, 3), (3, 3), (1, 2), (2, 1), (3, 2), (2, 3), (2, 2))
)
STAGES = (
    (0, 0, 8, 0, 0),
    (0, 128, 8, 0, 0),
    (0, 256, 16, 0, 0),
    (1, 0, 16, 1, 0),
    (2, 0, 16, 1, 1),
    (1, 256, 16, 1, 0),
    (2, 256, 16, 1, 1),
)
DIRECT = 3


def kernel(
    a_hbm,
    o_hbm,
    mine,
    rp,
    cp,
    dt,
    s_blk,
    u_blk,
    w_blk,
    lo,
    w,
    w_h,
    w_l,
    up,
    up_h,
    up_l,
    un_h,
    un_l,
    xr,
    xr_h,
    xr_l,
    xc_h,
    xc_l,
    io_sem,
    d1s,
    d1r,
    d2s,
    d2r,
    d3s,
    d3r,
    d4s,
    d4r,
    r1s,
    r2s,
    rr,
    cs,
    cr,
    c3s,
    c3r,
):
    r = lax.axis_index("row")
    q = lax.axis_index("col")
    z = r // 2
    core = lax.rem(r, 2)
    other = r + 1 - 2 * core
    x, y = q // 4, lax.rem(q, 4)
    u, v = x + core * (y - x), y + core * (x - y)

    def chip(u, v):
        return 4 * (u + core * (v - u)) + (v + core * (u - v))

    def around():
        for dx, dy in AROUND:
            yield lax.rem(x + dx, 4), lax.rem(y + dy, 4)

    def send(ref, send_sem, recv_sem, device):
        return pltpu.make_async_remote_copy(
            src_ref=ref,
            dst_ref=ref,
            send_sem=send_sem,
            recv_sem=recv_sem,
            device_id=device,
            device_id_type=MESH,
        )

    load = pltpu.make_async_copy(a_hbm, mine, io_sem.at[0])
    load.start()

    barrier = pltpu.get_barrier_semaphore()

    def greet(device):
        pl.semaphore_signal(barrier, inc=1, device_id=device, device_id_type=MESH)

    @pl.loop(1, J)
    def _(k):
        greet((r, lax.rem(q + k, J)))

    @pl.loop(1, Z)
    def _(k):
        greet((lax.rem(r + 2 * k, 2 * Z), q))

    greet((other, q))
    load.wait()

    def tile_col(i, m, b, count=T):
        return mine[pl.ds(i * T * 8 + m * 4 + b, count, stride=8), :]

    @pl.when(q < 2)
    def _():
        @pl.loop(0, 2)
        def _(i):
            for b in range(4):
                rp[q, pl.ds(pl.multiple_of(i * T, T), T), b * B : (b + 1) * B] = tile_col(i, 0, b)

    @pl.when(z == 0)
    def _():
        for m in range(2):
            for b in range(4):
                at = (m * 4 + b) * B
                cp[pl.ds(pl.multiple_of(core * T, T), T), at : at + B] = tile_col(0, m, b)

    for t, (dr, dq) in enumerate(((0, 0), (0, 1), (1, 1))):

        @pl.when((r == dr) & (q == dq))
        def _():
            for b in range(4):
                dt[t, :, b * B : (b + 1) * B] = tile_col(0, 0, b)

    pl.semaphore_wait(barrier, (J - 1) + (Z - 1) + 1)

    def start(copy):
        copy.start()

    def sent(copy):
        copy.wait_send()

    def piece(n, at, count=1):
        t, first, rows, _, _ = STAGES[n]
        return dt.at[t, pl.ds(pl.multiple_of(first + at * rows, 8), rows * count), :]

    def index(n, tx, ty):
        if n < DIRECT:
            return 4 * tx + ty
        return 4 * (ty + core * (tx - ty)) + (tx + core * (ty - tx))

    def d1(n, at, j):
        return send(piece(n, at), d1s.at[n, at], d1r.at[n], (r, j))

    def d2(n, k):
        return send(piece(n, index(n, x, y)), d2s.at[n, k], d2r.at[n], (2 * k + core, q))

    def d3(n, to, sender, j):
        return send(piece(n, sender), d3s.at[n, to], d3r.at[n, sender], (r, j))

    def d3u(n, to, sender, j):
        return send(piece(n, 4 * v + sender), d3s.at[n, to], d3r.at[n, sender], (r, j))

    def d3v(n, to, sender, j):
        return send(piece(n, 4 * sender, 4), d3s.at[n, 4 + to], d3r.at[n, 4 + sender], (r, j))

    def d4(n):
        return send(piece(n, 0, J), d4s.at[n], d4r.at[n], (other, q))

    def on_core(n):
        return core == STAGES[n][4]

    def is_source(n):
        return (z == 0) & (q == STAGES[n][3])

    def d_scatter(n, act):
        @pl.when(on_core(n) & is_source(n))
        def _():
            for tx, ty in around():
                act(d1(n, index(n, tx, ty), 4 * tx + ty))

    def d_along_z(n, act):
        @pl.when(on_core(n) & (z == 0))
        def _():
            for k in (4, 3, 5, 2, 6, 1, 7):
                act(d2(n, k))

    def d_step2(n):
        @pl.when(on_core(n) & (z == 0) & (q != STAGES[n][3]))
        def _():
            d1(n, index(n, x, y), q).wait_recv()

        d_along_z(n, start)

    def takes(n, j):
        return (z != 0) | (j != STAGES[n][3])

    def d_gather(n, act):
        @pl.when(on_core(n))
        def _():
            for tx, ty in around():
                j = 4 * tx + ty

                @pl.when(takes(n, j))
                def _():
                    act(d3(n, j, q, j))

    def d_gather_u(n, act):
        @pl.when(on_core(n))
        def _():
            for k in (1, 3, 2):
                to = lax.rem(u + k, 4)

                @pl.when(takes(n, chip(to, v)))
                def _():
                    act(d3u(n, to, u, chip(to, v)))

    def d_gather_v(n, act):
        @pl.when(on_core(n))
        def _():
            for k in (1, 3, 2):
                to = lax.rem(v + k, 4)

                @pl.when(takes(n, chip(u, to)))
                def _():
                    act(d3v(n, to, v, chip(u, to)))

    def d_step3(n):
        @pl.when(on_core(n) & (z != 0))
        def _():
            d2(n, 0).wait_recv()

        if n < DIRECT:
            d_gather(n, start)
        else:
            d_gather_u(n, start)

    def d_step3v(n):
        @pl.when(on_core(n) & jnp.logical_not(is_source(n)))
        def _():
            for k in (1, 3, 2):
                d3u(n, 0, lax.rem(u + k, 4), q).wait_recv()

        d_gather_v(n, start)

    def d_step4(n):
        @pl.when(on_core(n))
        def _():
            @pl.when(jnp.logical_not(is_source(n)))
            def _():
                if n < DIRECT:

                    @pl.loop(1, J)
                    def _(k):
                        d3(n, 0, lax.rem(q + k, J), q).wait_recv()

                else:
                    for k in (1, 3, 2):
                        d3v(n, 0, lax.rem(v + k, 4), q).wait_recv()

            d4(n).start()

        @pl.when(jnp.logical_not(on_core(n)))
        def _():
            d4(n).wait_recv()

    def d_finish(n):
        d_scatter(n, sent)
        d_along_z(n, sent)
        if n < DIRECT:
            d_gather(n, sent)
        else:
            d_gather_u(n, sent)
            d_gather_v(n, sent)

        @pl.when(on_core(n))
        def _():
            d4(n).wait_send()

    def r_stream(k):
        s, half = k // 2, k % 2
        way = 1 - 2 * half
        du = lax.rem(way * (u - core * s) + 8, 4)
        dv = lax.rem(way * (v - (1 - core) * s) + 8, 4)
        wrapped = (du == 0) & (dv > 0)
        depth = du + dv + jnp.where(wrapped, 4, 0)
        along_u = ((dv == 0) & (du < 3)) | ((dv > 0) & (du == 3))
        along_v = (du > 0) & (dv < 3)
        to_u = chip(lax.rem(u + way + 4, 4), v)
        to_v = chip(u, lax.rem(v + way + 4, 4))

        def copies(j):
            ref = rp.at[s, pl.ds(pl.multiple_of(half * T + j * 32, 32), 32), :]
            return [
                (along_u, send(ref, r1s.at[k, j], rr.at[k, j], (r, to_u))),
                (along_v, send(ref, r2s.at[k, j], rr.at[k, j], (r, to_v))),
            ]

        return depth, copies

    def c_stream(k):
        way = 1 - 2 * k
        depth = lax.rem(way * z + Z, Z)
        to = 2 * lax.rem(z + way + Z, Z) + core

        def copies(j):
            ref = cp.at[pl.ds(pl.multiple_of(core * T + k * 256 + j * 16, 16), 16), :]
            return [(depth < Z - 1, send(ref, cs.at[k, j], cr.at[k, j], (to, q)))]

        return depth, copies

    def c_share(half, k, part):
        ref = cp.at[pl.ds(pl.multiple_of(half * T + k * 256 + part * 64, 64), 64), :]
        return send(ref, c3s.at[k, part], c3r.at[k, part], (other, q))

    streams = [c_stream(0), c_stream(1)] + [r_stream(k) for k in range(4)]

    def tick(n):
        for k, (depth, copies) in enumerate(streams):
            j = n - LAG * depth

            @pl.when((j >= 0) & (j < CHUNKS))
            def _():
                @pl.when(depth > 0)
                def _():
                    copies(j)[0][1].wait_recv()

                for going, copy in copies(j):
                    pl.when(going)(copy.start)

                if k < 2:

                    @pl.when(lax.rem(j, 4) == 3)
                    def _():
                        c_share(core, k, j // 4).start()

    def c_arrive():
        @pl.loop(0, 4)
        def _(part):
            for k in range(2):
                c_share(1 - core, k, part).wait_recv()

    def streams_finish():
        @pl.loop(0, CHUNKS)
        def _(j):
            for _, copies in streams:
                for going, copy in copies(j):
                    pl.when(going)(copy.wait_send)

        @pl.loop(0, 4)
        def _(part):
            for k in range(2):
                c_share(core, k, part).wait_send()

    for n in range(len(STAGES)):
        d_scatter(n, start)
    for n in range(DIRECT):
        d_step2(n)
    for n in range(DIRECT):
        d_step3(n)
    for n in range(EARLY):
        tick(n)
    d_step2(3)
    d_step2(4)
    d_step4(0)

    services = {
        (0, 0): ((d_step2, 5), (d_step2, 6)),
        (0, 2): ((d_step3, 3), (d_step3, 4)),
        (0, 4): ((d_step4, 1),),
        (1, 1): ((d_step3v, 3), (d_step3v, 4)),
        (1, 2): ((d_step3, 5), (d_step3, 6)),
        (1, 4): ((d_step4, 2),),
        (2, 1): ((d_step3v, 5), (d_step3v, 6)),
        (2, 4): ((d_step4, 3), (d_step4, 4)),
        (3, 4): ((d_step4, 5), (d_step4, 6)),
    }

    lo[...] = jnp.zeros_like(lo)
    w[...] = jnp.zeros_like(w)

    @pl.loop(0, 2)
    def _(h):
        tile = 3 * h

        def between(k, t):
            tick(EARLY + 20 * h + 5 * k + t)
            if (k, t) in services:

                @pl.when(h == 0)
                def _():
                    for step, n in services[k, t]:
                        step(n)

        for k in range(4):
            at, end = k * B, (k + 1) * B
            rows = dt[tile, at:end, at:T]
            if k:
                left = split(lo[at:end, 0:at])
                rows = rows - dot3(left, split(up[0:at, at:T]))
            s_blk[...] = rows[:, 0:B]
            factor_block(s_blk, u_blk, w_blk, lambda t: between(k, t))
            w_kk = split(w_blk[...])
            w[h, at:end, at:end] = w_blk[...]
            if k:
                inner = dot3(left, split(w[h, 0:at, 0:at]))
                w[h, at:end, 0:at] = -dot3(w_kk, split(inner))
            if k < 3:
                beside = dot3(w_kk, split(rows[:, B:]))
                up[at:end, end:T] = beside
                lo[end:T, at:end] = beside.T

            between(k, 4)

        whole_w = split(w[h])
        w_h[h] = whole_w[0]
        w_l[h] = whole_w[1]

        @pl.when(h == 0)
        def _():
            over = dot3(whole_w, split(dt[1]))
            over_s = split(over)
            under_s = split(over.T)
            up_h[...], up_l[...] = over_s
            un_h[...], un_l[...] = under_s
            dt[3] = dt[2] - dot3(under_s, over_s)

    @pl.loop(EARLY + 40, CHUNKS + 7 * LAG)
    def _(n):
        tick(n)


    w0 = (w_h[0], w_l[0])
    w1 = (w_h[1], w_l[1])
    over = (up_h[...], up_l[...])
    under = (un_h[...], un_l[...])

    @pl.loop(0, 2)
    def _(i):
        rows = pl.ds(pl.multiple_of(i * T, T), T)
        x0 = dot3(split(rp[0, rows, :]), w0, NT)
        x0_s = split(x0)
        xr[rows, 0:T] = x0
        xr_h[rows, 0:T], xr_l[rows, 0:T] = x0_s
        rest = rp[1, rows, :] - dot3(x0_s, over)
        x1 = dot3(split(rest), w1, NT)
        xr[rows, T:] = x1
        xr_h[rows, T:], xr_l[rows, T:] = split(x1)

    c_arrive()

    @pl.loop(0, 2)
    def _(m):
        cols = pl.ds(pl.multiple_of(m * T, T), T)
        x0_s = split(dot3(w0, split(cp[0:T, cols])))
        xc_h[0:T, cols], xc_l[0:T, cols] = x0_s
        rest = cp[T:, cols] - dot3(under, x0_s)
        xc_h[T:, cols], xc_l[T:, cols] = split(dot3(w1, split(rest)))

    at_row = lax.broadcasted_iota(jnp.int32, (T, T), 0)
    at_col = lax.broadcasted_iota(jnp.int32, (T, T), 1)

    @pl.loop(0, 2)
    def _(i):
        rows = pl.ds(pl.multiple_of(i * T, T), T)

        def put(m, value, update):
            for b in range(4):
                place = pl.ds(i * T * 8 + m * 4 + b, T, stride=8)
                part = value[:, b * B : (b + 1) * B]
                mine[place, :] = mine[place, :] - part if update else part

        row_tile = r + J * i

        @pl.loop(0, 2)
        def _(m):
            cols = pl.ds(pl.multiple_of(m * T, T), T)
            col_tile = q + J * m

            @pl.when((col_tile >= 2) & (row_tile >= 2))
            def _():
                put(m, dot3((xr_h[rows, :], xr_l[rows, :]), (xc_h[:, cols], xc_l[:, cols])), True)

            @pl.when((col_tile >= 2) & (row_tile < 2))
            def _():
                put(m, jnp.zeros((T, T), F32), False)

            @pl.when(col_tile < 2)
            def _():
                value = xr[rows, pl.ds(pl.multiple_of(col_tile * T, T), T)]
                keep = (row_tile > col_tile) | ((row_tile == col_tile) & (at_row >= at_col))
                put(m, jnp.where(keep, value, 0.0), False)

        block = pl.ds(pl.multiple_of(i * T * 8, T * 8), T * 8)
        pltpu.make_async_copy(mine.at[block], o_hbm.at[block], io_sem.at[1 + i]).start()

    for n in range(len(STAGES)):
        d_finish(n)
    streams_finish()

    @pl.loop(0, 2)
    def _(i):
        block = pl.ds(pl.multiple_of(i * T * 8, T * 8), T * 8)
        pltpu.make_async_copy(mine.at[block], o_hbm.at[block], io_sem.at[1 + i]).wait()


def body(matrix):
    local = matrix.reshape(8192, 128)
    dma = pltpu.SemaphoreType.DMA
    out = pl.pallas_call(
        kernel,
        out_shape=jax.ShapeDtypeStruct((8192, 128), F32),
        in_specs=[pl.BlockSpec(memory_space=pl.ANY)],
        out_specs=pl.BlockSpec(memory_space=pl.ANY),
        scratch_shapes=[
            pltpu.VMEM((8192, 128), F32),
            pltpu.VMEM((2, 2 * T, T), F32),
            pltpu.VMEM((2 * T, 2 * T), F32),
            pltpu.VMEM((4, T, T), F32),
            pltpu.VMEM((B, B), F32),
            pltpu.VMEM((B, B), F32),
            pltpu.VMEM((B, B), F32),
            pltpu.VMEM((T, T), F32),
            pltpu.VMEM((2, T, T), F32),
            pltpu.VMEM((2, T, T), BF16),
            pltpu.VMEM((2, T, T), BF16),
            pltpu.VMEM((T, T), F32),
            pltpu.VMEM((T, T), BF16),
            pltpu.VMEM((T, T), BF16),
            pltpu.VMEM((T, T), BF16),
            pltpu.VMEM((T, T), BF16),
            pltpu.VMEM((2 * T, 2 * T), F32),
            pltpu.VMEM((2 * T, 2 * T), BF16),
            pltpu.VMEM((2 * T, 2 * T), BF16),
            pltpu.VMEM((2 * T, 2 * T), BF16),
            pltpu.VMEM((2 * T, 2 * T), BF16),
            dma((3,)),
            dma((7, J)),
            dma((7,)),
            dma((7, Z)),
            dma((7,)),
            dma((7, J)),
            dma((7, J)),
            dma((7,)),
            dma((7,)),
            dma((4, CHUNKS)),
            dma((4, CHUNKS)),
            dma((4, CHUNKS)),
            dma((2, CHUNKS)),
            dma((2, CHUNKS)),
            dma((2, 4)),
            dma((2, 4)),
        ],
        compiler_params=pltpu.CompilerParams(
            collective_id=0, has_side_effects=True, vmem_limit_bytes=56 * 1024 * 1024
        ),
        cost_estimate=pl.CostEstimate(
            flops=30_000_000_000, bytes_accessed=8 * 1024 * 1024, transcendentals=0
        ),
        name="panels",
    )(local)
    return out.reshape(matrix.shape)


def solution(mesh):
    return jax.shard_map(
        body,
        mesh=mesh,
        in_specs=(P(None, "row", None, None, "col", None),),
        out_specs=P(None, "row", None, None, "col", None),
        check_vma=False,
    )
```

```python
import jax
import jax.numpy as jnp
from jax import lax
from jax.experimental import pallas as pl
from jax.experimental.pallas import tpu as pltpu
from jax.sharding import PartitionSpec as P

F32 = jnp.float32
BF16 = jnp.bfloat16
MESH = pl.DeviceIdType.MESH
NN = (((1,), (0,)), ((), ()))
NT = (((1,), (1,)), ((), ()))
Z = 8
J = 16
T = 512
B = 128
CHUNKS = 16
LAG = 4
EARLY = 2


def split(x):
    high = x.astype(BF16)
    return high, (x - high.astype(F32)).astype(BF16)


def dot3(a, b, dims=NN):
    def one(x, y):
        return lax.dot_general(x, y, dims, preferred_element_type=F32)

    return one(a[0], b[0]) + (one(a[0], b[1]) + one(a[1], b[0]))


def times_lower(w, x):
    half = T // 2
    top = dot3([p[0:half, 0:half] for p in w], [p[0:half] for p in x])
    return jnp.concatenate([top, dot3([p[half:] for p in w], x)], 0)


def times_lower_transposed(x, w):
    half = T // 2
    left = dot3([p[:, 0:half] for p in x], [p[0:half, 0:half] for p in w], NT)
    return jnp.concatenate([left, dot3(x, [p[half:] for p in w], NT)], 1)


def lane(x, i):
    return jnp.take_along_axis(x, jnp.full((8, 128), i, jnp.int32), axis=1)


def sublane(x, i):
    return jnp.broadcast_to(x[i : i + 1, :], (8, 128))


def factor_block(s_ref, u_ref, w_ref, between):
    n = B // 8
    s = [s_ref[8 * i : 8 * i + 8, :] for i in range(n)]
    row = lax.broadcasted_iota(jnp.int32, (8, 128), 0)
    col = lax.broadcasted_iota(jnp.int32, (8, 128), 1)
    v = [(col == row + 8 * i).astype(F32) for i in range(n)]
    for g in range(n):
        if g % 4 == 0:
            between(g // 4)
        a = [sublane(s[g], j) for j in range(8)]
        x = [sublane(v[g], j) for j in range(8)]
        d = {}
        for i in range(8):
            for j in range(i + 1):
                d[i, j] = lane(a[j], 8 * g + i)
        inv = [None] * 8
        low = {}
        for j in range(8):
            inv[j] = 1.0 / d[j, j]
            for i in range(j + 1, 8):
                low[i, j] = d[i, j] * inv[j]
            for i in range(j + 1, 8):
                for k in range(j + 1, i + 1):
                    d[i, k] = d[i, k] - low[i, j] * d[k, j]
                a[i] = a[i] - low[i, j] * a[j]
                x[i] = x[i] - low[i, j] * x[j]
        scale = lax.rsqrt(d[7, 7])
        u_out = a[7] * scale
        w_out = x[7] * scale
        for j in range(7):
            scale = lax.rsqrt(d[j, j])
            u_out = jnp.where(row == j, a[j] * scale, u_out)
            w_out = jnp.where(row == j, x[j] * scale, w_out)
        u_ref[8 * g : 8 * g + 8, :] = jnp.where(col >= row + 8 * g, u_out, 0.0)
        w_ref[8 * g : 8 * g + 8, :] = w_out
        if g == n - 1:
            break
        y = [None] * 8
        p = [None] * 8
        for j in range(7, -1, -1):
            y[j] = a[j] * inv[j]
            p[j] = x[j] * inv[j]
            for i in range(7, j, -1):
                y[j] = y[j] - low[i, j] * y[i]
                p[j] = p[j] - low[i, j] * p[i]
        for r in range(g + 1, n):
            old = s[r]
            for j in range(7, -1, -1):
                c = lane(old, 8 * g + j)
                s[r] = s[r] - c * y[j]
                v[r] = v[r] - c * p[j]


AROUND = (
    ((1, 0), (0, 1), (3, 0), (0, 3), (1, 1), (0, 2), (3, 1), (2, 0))
    + ((1, 3), (3, 3), (1, 2), (2, 1), (3, 2), (2, 3), (2, 2))
)
STAGES = (
    (0, 0, 8, 0, 0),
    (0, 128, 8, 0, 0),
    (0, 256, 16, 0, 0),
    (1, 0, 16, 1, 0),
    (2, 0, 16, 1, 1),
    (1, 256, 16, 1, 0),
    (2, 256, 16, 1, 1),
)
DIRECT = 3


def kernel(
    a_hbm,
    xr_h_out,
    xr_l_out,
    xc_h_out,
    xc_l_out,
    mine,
    rp,
    cp,
    dt,
    s_blk,
    u_blk,
    w_blk,
    lo,
    w,
    w_h,
    w_l,
    up,
    up_h,
    up_l,
    un_h,
    un_l,
    xr_h,
    xr_l,
    xc_h,
    xc_l,
    io_sem,
    d1s,
    d1r,
    d2s,
    d2r,
    d3s,
    d3r,
    d4s,
    d4r,
    r1s,
    r2s,
    rr,
    cs,
    cr,
    c3s,
    c3r,
):
    r = lax.axis_index("row")
    q = lax.axis_index("col")
    z = r // 2
    core = lax.rem(r, 2)
    other = r + 1 - 2 * core
    x, y = q // 4, lax.rem(q, 4)
    u, v = x + core * (y - x), y + core * (x - y)

    def chip(u, v):
        return 4 * (u + core * (v - u)) + (v + core * (u - v))

    def around():
        for dx, dy in AROUND:
            yield lax.rem(x + dx, 4), lax.rem(y + dy, 4)

    def send(ref, send_sem, recv_sem, device):
        return pltpu.make_async_remote_copy(
            src_ref=ref,
            dst_ref=ref,
            send_sem=send_sem,
            recv_sem=recv_sem,
            device_id=device,
            device_id_type=MESH,
        )

    load = pltpu.make_async_copy(a_hbm, mine, io_sem.at[0])
    load.start()

    barrier = pltpu.get_barrier_semaphore()

    def greet(device):
        pl.semaphore_signal(barrier, inc=1, device_id=device, device_id_type=MESH)

    @pl.loop(1, J)
    def _(k):
        greet((r, lax.rem(q + k, J)))

    @pl.loop(1, Z)
    def _(k):
        greet((lax.rem(r + 2 * k, 2 * Z), q))

    greet((other, q))
    load.wait()

    def tile_col(i, m, b, count=T):
        return mine[pl.ds(i * T * 8 + m * 4 + b, count, stride=8), :]

    for t, (dr, dq) in enumerate(((0, 0), (0, 1), (1, 1))):

        @pl.when((r == dr) & (q == dq))
        def _():
            for b in range(4):
                dt[t, :, b * B : (b + 1) * B] = tile_col(0, 0, b)

    pl.semaphore_wait(barrier, (J - 1) + (Z - 1) + 1)

    def start(copy):
        copy.start()

    def sent(copy):
        copy.wait_send()

    def piece(n, at, count=1):
        t, first, rows, _, _ = STAGES[n]
        return dt.at[t, pl.ds(pl.multiple_of(first + at * rows, 8), rows * count), :]

    def index(n, tx, ty):
        if n < DIRECT:
            return 4 * tx + ty
        return 4 * (ty + core * (tx - ty)) + (tx + core * (ty - tx))

    def d1(n, at, j):
        return send(piece(n, at), d1s.at[n, at], d1r.at[n], (r, j))

    def d2(n, k):
        return send(piece(n, index(n, x, y)), d2s.at[n, k], d2r.at[n], (2 * k + core, q))

    def d3(n, to, sender, j):
        return send(piece(n, sender), d3s.at[n, to], d3r.at[n, sender], (r, j))

    def d3u(n, to, sender, j):
        return send(piece(n, 4 * v + sender), d3s.at[n, to], d3r.at[n, sender], (r, j))

    def d3v(n, to, sender, j):
        return send(piece(n, 4 * sender, 4), d3s.at[n, 4 + to], d3r.at[n, 4 + sender], (r, j))

    def d4(n):
        return send(piece(n, 0, J), d4s.at[n], d4r.at[n], (other, q))

    def on_core(n):
        return core == STAGES[n][4]

    def is_source(n):
        return (z == 0) & (q == STAGES[n][3])

    def d_scatter(n, act):
        @pl.when(on_core(n) & is_source(n))
        def _():
            for tx, ty in around():
                act(d1(n, index(n, tx, ty), 4 * tx + ty))

    def d_along_z(n, act):
        @pl.when(on_core(n) & (z == 0))
        def _():
            for k in (4, 3, 5, 2, 6, 1, 7):
                act(d2(n, k))

    def d_step2(n):
        @pl.when(on_core(n) & (z == 0) & (q != STAGES[n][3]))
        def _():
            d1(n, index(n, x, y), q).wait_recv()

        d_along_z(n, start)

    def takes(n, j):
        return (z != 0) | (j != STAGES[n][3])

    def d_gather(n, act):
        @pl.when(on_core(n))
        def _():
            for tx, ty in around():
                j = 4 * tx + ty

                @pl.when(takes(n, j))
                def _():
                    act(d3(n, j, q, j))

    def d_gather_u(n, act):
        @pl.when(on_core(n))
        def _():
            for k in (1, 3, 2):
                to = lax.rem(u + k, 4)

                @pl.when(takes(n, chip(to, v)))
                def _():
                    act(d3u(n, to, u, chip(to, v)))

    def d_gather_v(n, act):
        @pl.when(on_core(n))
        def _():
            for k in (1, 3, 2):
                to = lax.rem(v + k, 4)

                @pl.when(takes(n, chip(u, to)))
                def _():
                    act(d3v(n, to, v, chip(u, to)))

    def d_step3(n):
        @pl.when(on_core(n) & (z != 0))
        def _():
            d2(n, 0).wait_recv()

        if n < DIRECT:
            d_gather(n, start)
        else:
            d_gather_u(n, start)

    def d_step3v(n):
        @pl.when(on_core(n) & jnp.logical_not(is_source(n)))
        def _():
            for k in (1, 3, 2):
                d3u(n, 0, lax.rem(u + k, 4), q).wait_recv()

        d_gather_v(n, start)

    def d_step4(n):
        @pl.when(on_core(n))
        def _():
            @pl.when(jnp.logical_not(is_source(n)))
            def _():
                if n < DIRECT:

                    @pl.loop(1, J)
                    def _(k):
                        d3(n, 0, lax.rem(q + k, J), q).wait_recv()

                else:
                    for k in (1, 3, 2):
                        d3v(n, 0, lax.rem(v + k, 4), q).wait_recv()

            d4(n).start()

        @pl.when(jnp.logical_not(on_core(n)))
        def _():
            d4(n).wait_recv()

    def d_finish(n):
        d_scatter(n, sent)
        d_along_z(n, sent)
        if n < DIRECT:
            d_gather(n, sent)
        else:
            d_gather_u(n, sent)
            d_gather_v(n, sent)

        @pl.when(on_core(n))
        def _():
            d4(n).wait_send()

    def r_stream(k):
        s, half = k // 2, k % 2
        way = 1 - 2 * half
        du = lax.rem(way * (u - core * s) + 8, 4)
        dv = lax.rem(way * (v - (1 - core) * s) + 8, 4)
        wrapped = (du == 0) & (dv > 0)
        depth = du + dv + jnp.where(wrapped, 4, 0)
        along_u = ((dv == 0) & (du < 3)) | ((dv > 0) & (du == 3))
        along_v = (du > 0) & (dv < 3)
        to_u = chip(lax.rem(u + way + 4, 4), v)
        to_v = chip(u, lax.rem(v + way + 4, 4))

        def copies(j, count=1):
            ref = rp.at[s, pl.ds(pl.multiple_of(half * T + j * 32, 32), 32 * count), :]
            return [
                (along_u, send(ref, r1s.at[k], rr.at[k, j], (r, to_u))),
                (along_v, send(ref, r2s.at[k], rr.at[k, j], (r, to_v))),
            ]

        return depth, copies

    def c_stream(k):
        way = 1 - 2 * k
        depth = lax.rem(way * z + Z, Z)
        to = 2 * lax.rem(z + way + Z, Z) + core

        def copies(j, count=1):
            ref = cp.at[pl.ds(pl.multiple_of(core * T + k * 256 + j * 16, 16), 16 * count), :]
            return [(depth < Z - 1, send(ref, cs.at[k], cr.at[k, j], (to, q)))]

        return depth, copies

    def c_share(half, k, part, count=1):
        ref = cp.at[pl.ds(pl.multiple_of(half * T + k * 256 + part * 64, 64), 64 * count), :]
        return send(ref, c3s.at[k], c3r.at[k, part], (other, q))

    streams = [c_stream(0), c_stream(1)] + [r_stream(k) for k in range(4)]

    def tick(n):
        for k, (depth, copies) in enumerate(streams):
            j = n - LAG * depth

            @pl.when((j >= 0) & (j < CHUNKS))
            def _():
                @pl.when(depth > 0)
                def _():
                    copies(j)[0][1].wait_recv()

                for going, copy in copies(j):
                    pl.when(going)(copy.start)

                if k < 2:

                    @pl.when(lax.rem(j, 4) == 3)
                    def _():
                        c_share(core, k, j // 4).start()

    def c_arrive():
        @pl.loop(0, 4)
        def _(part):
            for k in range(2):
                c_share(1 - core, k, part).wait_recv()

    def streams_finish():
        for _, copies in streams:
            for going, copy in copies(0, CHUNKS):
                pl.when(going)(copy.wait_send)
        for k in range(2):
            c_share(core, k, 0, 4).wait_send()

    for n in range(len(STAGES)):
        d_scatter(n, start)

    @pl.when(q < 2)
    def _():
        @pl.loop(0, 2)
        def _(i):
            for b in range(4):
                rp[q, pl.ds(pl.multiple_of(i * T, T), T), b * B : (b + 1) * B] = tile_col(i, 0, b)

    @pl.when(z == 0)
    def _():
        for m in range(2):
            for b in range(4):
                at = (m * 4 + b) * B
                cp[pl.ds(pl.multiple_of(core * T, T), T), at : at + B] = tile_col(0, m, b)

    for n in range(DIRECT):
        d_step2(n)
    for n in range(DIRECT):
        d_step3(n)
    for n in range(EARLY):
        tick(n)
    d_step2(3)
    d_step2(4)
    d_step4(0)

    services = {
        (0, 0): ((d_step2, 5), (d_step2, 6)),
        (0, 1): ((d_step3, 3), (d_step3, 4)),
        (0, 3): ((d_step3v, 3), (d_step3v, 4)),
        (0, 4): ((d_step4, 1),),
        (1, 1): ((d_step3, 5), (d_step3, 6)),
        (1, 3): ((d_step3v, 5), (d_step3v, 6)),
        (1, 4): ((d_step4, 2),),
        (2, 2): ((d_step4, 3), (d_step4, 4)),
        (3, 2): ((d_step4, 5), (d_step4, 6)),
    }

    lo[...] = jnp.zeros_like(lo)
    w[...] = jnp.zeros_like(w)

    @pl.loop(0, 2)
    def _(h):
        tile = 3 * h

        def between(k, t):
            tick(EARLY + 20 * h + 5 * k + t)
            if (k, t) in services:

                @pl.when(h == 0)
                def _():
                    for step, n in services[k, t]:
                        step(n)

        for k in range(4):
            at, end = k * B, (k + 1) * B
            rows = dt[tile, at:end, at:T]
            if k:
                left = split(lo[at:end, 0:at])
                rows = rows - dot3(left, split(up[0:at, at:T]))
            s_blk[...] = rows[:, 0:B]
            factor_block(s_blk, u_blk, w_blk, lambda t: between(k, t))
            w_kk = split(w_blk[...])
            w[h, at:end, at:end] = w_blk[...]
            if k:
                inner = dot3(left, split(w[h, 0:at, 0:at]))
                w[h, at:end, 0:at] = -dot3(w_kk, split(inner))
            if k < 3:
                beside = dot3(w_kk, split(rows[:, B:]))
                up[at:end, end:T] = beside
                lo[end:T, at:end] = beside.T

            between(k, 4)

        whole_w = split(w[h])
        w_h[h] = whole_w[0]
        w_l[h] = whole_w[1]

        @pl.when(h == 0)
        def _():
            over = dot3(whole_w, split(dt[1]))
            over_s = split(over)
            under_s = split(over.T)
            up_h[...], up_l[...] = over_s
            un_h[...], un_l[...] = under_s
            dt[3] = dt[2] - dot3(under_s, over_s)

    @pl.loop(EARLY + 40, CHUNKS + 7 * LAG)
    def _(n):
        tick(n)


    w0 = (w_h[0], w_l[0])
    w1 = (w_h[1], w_l[1])
    over = (up_h[...], up_l[...])
    under = (un_h[...], un_l[...])

    @pl.loop(0, 2)
    def _(i):
        rows = pl.ds(pl.multiple_of(i * T, T), T)
        x0 = times_lower_transposed(split(rp[0, rows, :]), w0)
        x0_s = split(x0)
        xr_h[rows, 0:T], xr_l[rows, 0:T] = x0_s
        rest = rp[1, rows, :] - dot3(x0_s, over)
        x1 = times_lower_transposed(split(rest), w1)
        xr_h[rows, T:], xr_l[rows, T:] = split(x1)

    results = ((xr_h, xr_h_out), (xr_l, xr_l_out), (xc_h, xc_h_out), (xc_l, xc_l_out))
    for n, (source, out) in enumerate(results[:2]):
        pltpu.make_async_copy(source, out, io_sem.at[1 + n]).start()

    c_arrive()

    @pl.loop(0, 2)
    def _(m):
        cols = pl.ds(pl.multiple_of(m * T, T), T)
        x0_s = split(times_lower(w0, split(cp[0:T, cols])))
        xc_h[0:T, cols], xc_l[0:T, cols] = x0_s
        rest = cp[T:, cols] - dot3(under, x0_s)
        xc_h[T:, cols], xc_l[T:, cols] = split(times_lower(w1, split(rest)))

    for n, (source, out) in enumerate(results[2:], 2):
        pltpu.make_async_copy(source, out, io_sem.at[1 + n]).start()

    for n in range(len(STAGES)):
        d_finish(n)
    streams_finish()

    for n, (source, out) in enumerate(results):
        pltpu.make_async_copy(source, out, io_sem.at[1 + n]).wait()


def update(xr_h, xr_l, xc_h, xc_l, a_ref, o_ref):
    row_tile = lax.axis_index("row") + J * pl.program_id(0)
    q = lax.axis_index("col")

    for m in range(2):
        cols = slice(m * T, (m + 1) * T)
        col_tile = q + J * m

        def put(value, subtract):
            for b in range(4):
                place = pl.ds(m * 4 + b, T, stride=8)
                part = value[:, b * B : (b + 1) * B]
                o_ref[place, :] = a_ref[place, :] - part if subtract else part

        @pl.when((col_tile >= 2) & (row_tile >= 2))
        def _():
            put(dot3((xr_h[...], xr_l[...]), (xc_h[:, cols], xc_l[:, cols])), True)

        @pl.when((col_tile >= 2) & (row_tile < 2))
        def _():
            put(jnp.zeros((T, T), F32), False)

        if m == 0:

            @pl.when(col_tile < 2)
            def _():
                place = pl.ds(pl.multiple_of(col_tile * T, T), T)
                value = xr_h[:, place].astype(F32) + xr_l[:, place].astype(F32)
                at_row = lax.broadcasted_iota(jnp.int32, (T, T), 0)
                at_col = lax.broadcasted_iota(jnp.int32, (T, T), 1)
                keep = (row_tile > col_tile) | ((row_tile == col_tile) & (at_row >= at_col))
                put(jnp.where(keep, value, 0.0), False)


def body(matrix):
    local = matrix.reshape(8192, 128)
    dma = pltpu.SemaphoreType.DMA
    panels = pl.pallas_call(
        kernel,
        out_shape=[jax.ShapeDtypeStruct((2 * T, 2 * T), BF16)] * 4,
        in_specs=[pl.BlockSpec(memory_space=pl.ANY)],
        out_specs=[pl.BlockSpec(memory_space=pl.ANY)] * 4,
        scratch_shapes=[
            pltpu.VMEM((8192, 128), F32),
            pltpu.VMEM((2, 2 * T, T), F32),
            pltpu.VMEM((2 * T, 2 * T), F32),
            pltpu.VMEM((4, T, T), F32),
            pltpu.VMEM((B, B), F32),
            pltpu.VMEM((B, B), F32),
            pltpu.VMEM((B, B), F32),
            pltpu.VMEM((T, T), F32),
            pltpu.VMEM((2, T, T), F32),
            pltpu.VMEM((2, T, T), BF16),
            pltpu.VMEM((2, T, T), BF16),
            pltpu.VMEM((T, T), F32),
            pltpu.VMEM((T, T), BF16),
            pltpu.VMEM((T, T), BF16),
            pltpu.VMEM((T, T), BF16),
            pltpu.VMEM((T, T), BF16),
            pltpu.VMEM((2 * T, 2 * T), BF16),
            pltpu.VMEM((2 * T, 2 * T), BF16),
            pltpu.VMEM((2 * T, 2 * T), BF16),
            pltpu.VMEM((2 * T, 2 * T), BF16),
            dma((5,)),
            dma((7, J)),
            dma((7,)),
            dma((7, Z)),
            dma((7,)),
            dma((7, J)),
            dma((7, J)),
            dma((7,)),
            dma((7,)),
            dma((4,)),
            dma((4,)),
            dma((4, CHUNKS)),
            dma((2,)),
            dma((2, CHUNKS)),
            dma((2,)),
            dma((2, 4)),
        ],
        compiler_params=pltpu.CompilerParams(
            collective_id=0, has_side_effects=True, vmem_limit_bytes=56 * 1024 * 1024
        ),
        cost_estimate=pl.CostEstimate(
            flops=30_000_000_000, bytes_accessed=8 * 1024 * 1024, transcendentals=0
        ),
        name="panels",
    )(local)
    out = pl.pallas_call(
        update,
        grid=(2,),
        out_shape=jax.ShapeDtypeStruct((8192, 128), F32),
        in_specs=[pl.BlockSpec((T, 2 * T), lambda i: (i, 0))] * 2
        + [pl.BlockSpec((2 * T, 2 * T), lambda i: (0, 0))] * 2
        + [pl.BlockSpec((T * 8, 128), lambda i: (i, 0))],
        out_specs=pl.BlockSpec((T * 8, 128), lambda i: (i, 0)),
        compiler_params=pltpu.CompilerParams(vmem_limit_bytes=60 * 1024 * 1024),
        cost_estimate=pl.CostEstimate(
            flops=6_400_000_000, bytes_accessed=16 * 1024 * 1024, transcendentals=0
        ),
        name="update",
    )(*panels, local)
    return out.reshape(matrix.shape)


def solution(mesh):
    return jax.shard_map(
        body,
        mesh=mesh,
        in_specs=(P(None, "row", None, None, "col", None),),
        out_specs=P(None, "row", None, None, "col", None),
        check_vma=False,
    )
```
